512 devices in a mesh: dp: 16 (over z, core), tp: 32 (over x, y).
Axes of the slice: x: 4, y: 8, z: 8, core: 2. Of those that a mesh axis runs over, the one named last changes fastest.
Arguments:
- queries: bfloat16 [4096, 36864], P(('dp', 'tp')), parts along dimension 0
- cache_latent: bfloat16 [131072, 576], P(('dp', 'tp')), parts along dimension 0
- row_counts: int32 [512], P(('dp', 'tp')), parts along dimension 0, may hold values from 4 to 8, as said below
- row_kinds: int32 [4096], P(('dp', 'tp')), parts along dimension 0, may hold values from 0 to 1
- cache_lengths: int32 [4096], P(('dp', 'tp')), parts along dimension 0, may hold values from 1 to 128
- positions: int32 [4096], P(('dp', 'tp')), parts along dimension 0, may hold values from 0 to 127
- hidden_units: bfloat16 [4096, 9216], P('dp', 'tp'), parts along dimension 0, may hold values from -6 to 6
- down_proj: bfloat16 [9216, 3584], P('tp'), may hold values from -0.0625 to 0.0625
Outputs:
- attended: bfloat16 [4096, 32768], P(('dp', 'tp')), parts along dimension 0
- ffn_out: bfloat16 [4096, 3584], P(('dp', 'tp')), parts along dimension 0
The draws below stay inside these ranges and needn't reach their ends.
There are 16 independent parts, one for each index of `dp`. The reference program is written for one: setup_inputs(seed, part) draws one part's arguments, and reference() takes and returns one part's arrays. A program takes and returns all parts, laid end to end along the dimension named above; an argument that names none is the same for every part. Nothing has to cross between parts.
Inputs may be any that keep to these rules, and one draw needn't show every extreme that they name: `row_counts`: every device has at least 4 live rows; some device has all 8 slots live.
All inputs are finite; a program needn't handle non-finite values.
Results may differ from the reference program's by a relative error of at most 0.02.
Values may be sent and summed in bfloat16 or wider, within the bound.
No kernel may reach another device: no remote copies, remote signals or barrier semaphores. Data moves between devices by JAX's collectives and lax.ppermute only.
A program may use at most 64 MiB of HBM per device.

```python
import jax
import jax.numpy as jnp
from jax import lax

D = 3584
FF_DEV = 288
HEADS = 64
KVL = 512
QK_DIM = 192
ROWS = 8
CACHE = 256
LAT = 576
FF = 9216
ROWS_ALL = 256
CACHE_ALL = 8192
N_TP = 32


def latent_base(key):
    return jnp.clip(jax.random.normal(key, (CACHE_ALL, LAT), jnp.float32), -6.0, 6.0)


def draw_cache_latent(key, part):
    base = latent_base(key)
    return base.astype(jnp.bfloat16)


def draw_queries(key, part):
    key = jax.random.fold_in(key, 23)
    noise = jnp.clip(jax.random.normal(key, (ROWS_ALL, HEADS, LAT), jnp.float32), -6.0, 6.0)
    return noise.reshape(ROWS_ALL, HEADS * LAT).astype(jnp.bfloat16)


def draw_row_counts(key, part):
    key = jax.random.fold_in(key, 5)
    first_key, second_key = jax.random.split(key)
    counts = jax.random.randint(first_key, (N_TP,), 4, ROWS + 1)
    fullest = jax.random.randint(second_key, (), 0, N_TP)
    return jnp.where(jnp.arange(N_TP) == fullest, ROWS, counts).astype(jnp.int32)


def plant(result, rng, low, top_value):
    dims = result.shape
    spot = [jax.random.randint(jax.random.fold_in(rng, axis), (), 0, dims[axis]) for axis in range(len(dims))]
    result = result.at[tuple(spot)].set(low)
    longest = dims.index(max(dims))
    spot[longest] = (spot[longest] + 1) % dims[longest]
    return result.at[tuple(spot)].set(top_value)


def block_levels(key, extent, shards, low, top_value):
    def one(position, parts):
        steps = jax.random.uniform(jax.random.fold_in(jax.random.fold_in(key, 6), position), (parts,), jnp.float32, low / len(shards), top_value / len(shards))
        return jnp.repeat(jnp.exp(steps), extent[position] // parts).reshape((-1,) + (1,) * (len(extent) - position - 1))

    loudness = one(*shards[0])
    for cut in shards[1:]:
        loudness = loudness * one(*cut)
    return loudness


def scatter_about(own_key, shape, deviation, reach, shards=(), kind=jnp.bfloat16):
    result = deviation * jax.random.normal(own_key, shape, jnp.float32)
    if shards:
        result = result * block_levels(own_key, shape, shards, -0.22, 0.18)
    return jnp.clip(result, -reach, reach).astype(kind)


def setup_inputs(seed: int = 0, part: int = 0) -> dict:
    key_list = jax.random.split(jax.random.key(seed), 9)
    part_splits = jax.random.split(jax.random.fold_in(key_list[8], part), 9)
    queries = draw_queries(jax.random.fold_in(jax.random.fold_in(key_list[8], part), 71), part)
    cache_latent = draw_cache_latent(jax.random.fold_in(jax.random.fold_in(key_list[8], part), 71), part)
    row_counts = draw_row_counts(jax.random.fold_in(jax.random.fold_in(key_list[8], part), 71), part)
    row_kinds = plant(jax.random.randint(part_splits[3], (ROWS_ALL,), 0, 2), jax.random.fold_in(part_splits[3], 1), 0, 1).astype(jnp.int32)
    cache_lengths = plant(jax.random.randint(part_splits[4], (ROWS_ALL,), 1, CACHE // 2 + 1), jax.random.fold_in(part_splits[4], 1), 1, (CACHE // 2 + 1) - 1).astype(jnp.int32)
    positions = plant(jax.random.randint(part_splits[5], (ROWS_ALL,), 0, CACHE // 2), jax.random.fold_in(part_splits[5], 1), 0, (CACHE // 2) - 1).astype(jnp.int32)
    hidden_units = scatter_about(part_splits[6], (ROWS_ALL, FF), 1.0, 6.0, ((1, 32),))
    down_proj = scatter_about(key_list[7], (FF, D), FF ** -0.5, 0.0625, ((0, 32),))
    return dict(queries=queries, cache_latent=cache_latent, row_counts=row_counts, row_kinds=row_kinds, cache_lengths=cache_lengths, positions=positions, hidden_units=hidden_units, down_proj=down_proj)


def attend_block(query_rows, cache_rows, lengths, offsets, kinds, count):
    scale = QK_DIM ** -0.5
    query_rows = query_rows.reshape(ROWS, HEADS, LAT).astype(jnp.float32)
    keys = cache_rows.astype(jnp.float32)
    scores = jnp.einsum("rhd,kd->rhk", query_rows, keys) * scale
    index = jnp.arange(CACHE, dtype=jnp.int32)[None, :]
    top_entry = (lengths + offsets)[:, None]
    causal = index <= top_entry
    verify = (index < lengths[:, None]) | (index == top_entry)
    allowed = jnp.where(kinds[:, None] == 1, verify, causal)[:, None, :]
    masked = jnp.where(allowed, scores, jnp.float32(-1e30))
    peak = jnp.max(masked, axis=-1, keepdims=True)
    expo = jnp.where(allowed, jnp.exp(masked - peak), jnp.float32(0.0))
    probs = (expo / jnp.sum(expo, axis=-1, keepdims=True)).astype(jnp.bfloat16)
    values = cache_rows[:, :KVL].astype(jnp.float32)
    output = jnp.einsum("rhk,kd->rhd", probs.astype(jnp.float32), values)
    alive = jnp.arange(ROWS, dtype=jnp.int32) < count
    output = jnp.where(alive[:, None, None], output, jnp.float32(0.0))
    return output.astype(jnp.bfloat16).reshape(ROWS, HEADS * KVL)


def reference(queries, cache_latent, row_counts, row_kinds, cache_lengths, positions, hidden_units, down_proj):
    attended = lax.map(
        lambda items: attend_block(*items),
        (queries.reshape(N_TP, ROWS, HEADS * LAT), cache_latent.reshape(N_TP, CACHE, LAT),
         cache_lengths.reshape(N_TP, ROWS), positions.reshape(N_TP, ROWS),
         row_kinds.reshape(N_TP, ROWS), row_counts))
    attended = attended.reshape(ROWS_ALL, HEADS * KVL)
    slot = jnp.arange(ROWS_ALL, dtype=jnp.int32) % ROWS
    alive = slot < jnp.repeat(row_counts, ROWS)
    masked = jnp.where(alive[:, None], hidden_units, jnp.zeros_like(hidden_units))

    def add_block(total, block):
        start = (block * FF_DEV).astype(jnp.int32)
        units = lax.dynamic_slice_in_dim(masked, start, FF_DEV, 1)
        weights_down = lax.dynamic_slice_in_dim(down_proj, start, FF_DEV, 0)
        partial_value = jnp.dot(units, weights_down, preferred_element_type=jnp.float32).astype(jnp.bfloat16)
        partial_value = lax.optimization_barrier(partial_value)
        return total + partial_value.astype(jnp.float32), None

    total, _ = lax.scan(add_block, jnp.zeros((ROWS_ALL, D), jnp.float32), jnp.arange(N_TP, dtype=jnp.int32))
    return attended, total.astype(jnp.bfloat16)
```

```python
import jax
import jax.numpy as jnp
from jax import lax
from jax.sharding import PartitionSpec as P

HEADS = 64
KVL = 512
QK_DIM = 192
LAT = 576
X_RING = 4
Y_RING = 8


def attend_local(queries, cache_latent, lengths, offsets, kinds, alive):
    row_total = queries.shape[0]
    entries = cache_latent.shape[0]
    scale = QK_DIM ** (-0.5)
    query_rows = queries.reshape(row_total, HEADS, LAT)
    scores = (
        jnp.einsum("rhd,kd->rhk", query_rows, cache_latent, preferred_element_type=jnp.float32)
        * scale
    )
    index = lax.broadcasted_iota(jnp.int32, (1, entries), 1)
    top_entry = (lengths + offsets)[:, None]
    causal = index <= top_entry
    verify = (index < lengths[:, None]) | (index == top_entry)
    allowed = jnp.where(kinds[:, None] == 1, verify, causal)[:, None, :]
    masked = jnp.where(allowed, scores, jnp.float32(-1e30))
    peak = jnp.max(masked, axis=-1, keepdims=True)
    expo = jnp.where(allowed, jnp.exp(masked - peak), jnp.float32(0.0))
    probs = (expo / jnp.sum(expo, axis=-1, keepdims=True)).astype(jnp.bfloat16)
    output = jnp.einsum(
        "rhk,kd->rhd", probs, cache_latent[:, :KVL], preferred_element_type=jnp.float32
    )
    output = jnp.where(alive[:, None, None], output, jnp.float32(0.0))
    return output.astype(jnp.bfloat16).reshape(row_total, HEADS * KVL)


def member(block, kind):
    return 2 * block + ((kind ^ block) & 1)


def device(group, x, y):
    shift = group % 2
    return group * X_RING * Y_RING + (x + shift) % X_RING * Y_RING + (y + shift) % Y_RING


def block_groups(groups):
    return [
        [device(g, member(bx, sx), member(by, sy)) for sx in range(2) for sy in range(2)]
        for g in range(groups)
        for bx in range(X_RING // 2)
        for by in range(Y_RING // 2)
    ]


def kind_groups(groups):
    return [
        [
            device(g, member(bx, sx), member(by, sy))
            for bx in range(X_RING // 2)
            for by in range(Y_RING // 2)
        ]
        for g in range(groups)
        for sx in range(2)
        for sy in range(2)
    ]


def row_order(rows, total, shift):
    index = lax.broadcasted_iota(jnp.int32, (total,), 0)
    slot, block = index % rows, index // rows
    sx, sy, bx, by = block // 16, block // 8 % 2, block // 4 % 2, block % 4
    x, y = member(bx, sx), member(by, sy)
    return ((x + shift) % X_RING * Y_RING + (y + shift) % Y_RING) * rows + slot


def exchange(values, groups):
    parts = len(groups[0])
    moved = lax.all_to_all(
        values, ("dp", "tp"), 0, 0, tiled=True, axis_index_groups=groups
    ).reshape(parts, values.shape[0] // parts, values.shape[1])
    return jnp.sum(moved.astype(jnp.float32), axis=0)


def solution(mesh):
    groups = mesh.shape["dp"]

    def shards(
        queries, cache_latent, row_counts, row_kinds, cache_lengths, positions, hidden_units, down_proj
    ):
        row_total = queries.shape[0]
        alive = lax.broadcasted_iota(jnp.int32, (row_total,), 0) < row_counts[0]
        attended = attend_local(queries, cache_latent, cache_lengths, positions, row_kinds, alive)
        total = hidden_units.shape[0]
        order = row_order(row_total, total, lax.axis_index("dp") % 2)
        pick = (order[:, None] == lax.broadcasted_iota(jnp.int32, (total, total), 1)).astype(
            jnp.bfloat16
        )
        ordered = jnp.dot(pick, hidden_units, preferred_element_type=jnp.float32).astype(
            jnp.bfloat16
        )
        partial_value = jnp.dot(ordered, down_proj, preferred_element_type=jnp.float32)
        quarter = exchange(partial_value.astype(jnp.bfloat16), block_groups(groups))
        summed = exchange(quarter.astype(jnp.bfloat16), kind_groups(groups))
        summed = jnp.where(alive[:, None], summed, jnp.float32(0.0)).astype(jnp.bfloat16)
        return (attended, summed)

    placed = (
        P(("dp", "tp"), None),
        P(("dp", "tp"), None),
        P(("dp", "tp")),
        P(("dp", "tp")),
        P(("dp", "tp")),
        P(("dp", "tp")),
        P("dp", "tp"),
        P("tp", None),
    )
    return jax.shard_map(
        shards,
        mesh=mesh,
        in_specs=placed,
        out_specs=(P(("dp", "tp"), None), P(("dp", "tp"), None)),
        check_vma=False,
    )
```

```python
import functools

import jax
import jax.numpy as jnp
from jax import lax
from jax.experimental import pallas as pl
from jax.experimental.pallas import tpu as pltpu
from jax.sharding import PartitionSpec as P

HEADS = 64
KVL = 512
QK_DIM = 192
LAT = 576
X_RING = 4
Y_RING = 8
CUTS = (0, 3584)
TILE = 896


def attend_local(queries, cache_latent, lengths, offsets, kinds, alive):
    row_total = queries.shape[0]
    entries = cache_latent.shape[0]
    scale = QK_DIM ** (-0.5)
    query_rows = queries.reshape(row_total, HEADS, LAT)
    scores = (
        jnp.einsum("rhd,kd->rhk", query_rows, cache_latent, preferred_element_type=jnp.float32)
        * scale
    )
    index = lax.broadcasted_iota(jnp.int32, (1, entries), 1)
    top_entry = (lengths + offsets)[:, None]
    causal = index <= top_entry
    verify = (index < lengths[:, None]) | (index == top_entry)
    allowed = jnp.where(kinds[:, None] == 1, verify, causal)[:, None, :]
    masked = jnp.where(allowed, scores, jnp.float32(-1e30))
    peak = jnp.max(masked, axis=-1, keepdims=True)
    expo = jnp.where(allowed, jnp.exp(masked - peak), jnp.float32(0.0))
    probs = (expo / jnp.sum(expo, axis=-1, keepdims=True)).astype(jnp.bfloat16)
    output = jnp.einsum(
        "rhk,kd->rhd", probs, cache_latent[:, :KVL], preferred_element_type=jnp.float32
    )
    output = jnp.where(alive[:, None, None], output, jnp.float32(0.0))
    return output.astype(jnp.bfloat16).reshape(row_total, HEADS * KVL)


def member(block, kind):
    return 2 * block + ((kind ^ block) & 1)


def device(group, x, y):
    shift = group % 2
    return group * X_RING * Y_RING + (x + shift) % X_RING * Y_RING + (y + shift) % Y_RING


def block_groups(groups):
    return [
        [device(g, member(bx, sx), member(by, sy)) for sx in range(2) for sy in range(2)]
        for g in range(groups)
        for bx in range(X_RING // 2)
        for by in range(Y_RING // 2)
    ]


def kind_groups(groups):
    return [
        [
            device(g, member(bx, sx), member(by, sy))
            for bx in range(X_RING // 2)
            for by in range(Y_RING // 2)
        ]
        for g in range(groups)
        for sx in range(2)
        for sy in range(2)
    ]


def row_order(index, shift):
    slot, block = index & 7, index >> 3
    sx, sy, bx, by = block >> 4, (block >> 3) & 1, (block >> 2) & 1, block & 3
    x, y = member(bx, sx), member(by, sy)
    return ((((x + shift) & 3) << 3) + ((y + shift) & 7)) * 8 + slot


def partial_kernel(tile, shift_ref, units_hbm, down_hbm, out_ref, units, down, sems):
    tiles = down.shape[0]
    unit_copy = pltpu.make_async_copy(units_hbm, units, sems.at[tiles])
    unit_copy.start()
    copies = [
        pltpu.make_async_copy(down_hbm.at[:, pl.ds(j * tile, tile)], down.at[j], sems.at[j])
        for j in range(tiles)
    ]
    for copy in copies:
        copy.start()
    total = units.shape[1]
    order = row_order(lax.broadcasted_iota(jnp.int32, (total, total), 0), shift_ref[0])
    pick = order == lax.broadcasted_iota(jnp.int32, (total, total), 1)
    pick = jnp.where(pick, 1.0, 0.0).astype(jnp.bfloat16)
    unit_copy.wait()
    ordered = lax.dot_general(
        pick, units[...], (((1,), (1,)), ((), ())), preferred_element_type=jnp.float32
    ).astype(jnp.bfloat16)
    for j, copy in enumerate(copies):
        copy.wait()
        out_ref[:, pl.ds(j * tile, tile)] = jnp.dot(
            ordered, down[j], preferred_element_type=jnp.float32
        ).astype(jnp.bfloat16)


def partial_sums(shift, units_t, down_proj):
    units, total = units_t.shape
    width = down_proj.shape[1]
    tiles = width // TILE
    return pl.pallas_call(
        functools.partial(partial_kernel, TILE),
        out_shape=jax.ShapeDtypeStruct((total, width), jnp.bfloat16),
        in_specs=[
            pl.BlockSpec(memory_space=pltpu.SMEM),
            pl.BlockSpec(memory_space=pl.ANY),
            pl.BlockSpec(memory_space=pl.ANY),
        ],
        out_specs=pl.BlockSpec(memory_space=pltpu.VMEM),
        scratch_shapes=[
            pltpu.VMEM((units, total), jnp.bfloat16),
            pltpu.VMEM((tiles, units, TILE), jnp.bfloat16),
            pltpu.SemaphoreType.DMA((tiles + 1,)),
        ],
        compiler_params=pltpu.CompilerParams(vmem_limit_bytes=56 * 2**20),
        cost_estimate=pl.CostEstimate(
            flops=2 * total * units * width,
            bytes_accessed=2 * (units * (width + total) + total * width),
            transcendentals=0,
        ),
        name="partial_sums",
    )(shift, units_t, down_proj)


def sum_kernel(parts, in_ref, out_ref):
    rows = out_ref.shape[0]
    value = in_ref[pl.ds(0, rows), :].astype(jnp.float32)
    for part in range(1, parts):
        value += in_ref[pl.ds(part * rows, rows), :].astype(jnp.float32)
    out_ref[...] = value.astype(jnp.bfloat16)


def sum_parts(values, parts):
    rows, width = values.shape[0] // parts, values.shape[1]
    return pl.pallas_call(
        functools.partial(sum_kernel, parts),
        out_shape=jax.ShapeDtypeStruct((rows, width), jnp.bfloat16),
        compiler_params=pltpu.CompilerParams(vmem_limit_bytes=16 * 2**20),
        cost_estimate=pl.CostEstimate(
            flops=values.size, bytes_accessed=2 * (values.size + rows * width), transcendentals=0
        ),
        name="sum_parts",
    )(values)


def final_kernel(count_ref, *refs):
    out_ref = refs[-1]
    rows = out_ref.shape[0]
    for (start, stop), ref in zip(zip(CUTS[:-1], CUTS[1:]), refs[:-1]):
        value = jnp.zeros((rows, stop - start), jnp.float32)
        for pair in range(0, ref.shape[0], 2 * rows):
            both = ref[pl.ds(pair, 2 * rows), :].astype(jnp.float32)
            value += both[:rows] + both[rows:]
        row = lax.broadcasted_iota(jnp.int32, value.shape, 0)
        value = jnp.where(row < count_ref[0], value, 0.0)
        out_ref[:, pl.ds(start, stop - start)] = value.astype(jnp.bfloat16)


def final_sum(counts, halves, rows):
    return pl.pallas_call(
        final_kernel,
        out_shape=jax.ShapeDtypeStruct((rows, CUTS[-1]), jnp.bfloat16),
        in_specs=[pl.BlockSpec(memory_space=pltpu.SMEM)]
        + [pl.BlockSpec(memory_space=pltpu.VMEM) for _ in halves],
        compiler_params=pltpu.CompilerParams(vmem_limit_bytes=16 * 2**20),
        name="final_sum",
    )(counts, *halves)


def exchange(values, groups):
    return lax.all_to_all(values, ("dp", "tp"), 0, 0, tiled=True, axis_index_groups=groups)


def solution(mesh):
    groups = mesh.shape["dp"]

    def shards(
        queries, cache_latent, row_counts, row_kinds, cache_lengths, positions, hidden_units, down_proj
    ):
        row_total = queries.shape[0]
        alive = lax.broadcasted_iota(jnp.int32, (row_total,), 0) < row_counts[0]
        shift = (lax.axis_index("dp") % 2).astype(jnp.int32).reshape(1)
        part = partial_sums(shift, hidden_units.T, down_proj)
        moved = exchange(part, block_groups(groups))
        attended = attend_local(queries, cache_latent, cache_lengths, positions, row_kinds, alive)
        moved, attended = lax.optimization_barrier((moved, attended))
        quarter = sum_parts(moved, 4)
        moved = exchange(quarter, kind_groups(groups))
        summed = final_sum(row_counts, [moved], row_total)
        return (attended, summed)

    placed = (
        P(("dp", "tp"), None),
        P(("dp", "tp"), None),
        P(("dp", "tp")),
        P(("dp", "tp")),
        P(("dp", "tp")),
        P(("dp", "tp")),
        P("dp", "tp"),
        P("tp", None),
    )
    return jax.shard_map(
        shards,
        mesh=mesh,
        in_specs=placed,
        out_specs=(P(("dp", "tp"), None), P(("dp", "tp"), None)),
        check_vma=False,
    )
```

```python
import functools

import jax
import jax.numpy as jnp
from jax import lax
from jax.experimental import pallas as pl
from jax.experimental.pallas import tpu as pltpu
from jax.sharding import PartitionSpec as P

HEADS = 64
KVL = 512
QK_DIM = 192
LAT = 576
X_RING = 4
Y_RING = 8
CUTS = (0, 3584)
TILE = 896


def attend_local(queries, cache_latent, lengths, offsets, kinds, alive):
    row_total = queries.shape[0]
    entries = cache_latent.shape[0]
    scale = QK_DIM ** (-0.5)
    query_rows = queries.reshape(row_total, HEADS, LAT)
    scores = (
        jnp.einsum("rhd,kd->rhk", query_rows, cache_latent, preferred_element_type=jnp.float32)
        * scale
    )
    index = lax.broadcasted_iota(jnp.int32, (1, entries), 1)
    top_entry = (lengths + offsets)[:, None]
    causal = index <= top_entry
    verify = (index < lengths[:, None]) | (index == top_entry)
    allowed = jnp.where(kinds[:, None] == 1, verify, causal)[:, None, :]
    masked = jnp.where(allowed, scores, jnp.float32(-1e30))
    peak = jnp.max(masked, axis=-1, keepdims=True)
    expo = jnp.where(allowed, jnp.exp(masked - peak), jnp.float32(0.0))
    probs = (expo / jnp.sum(expo, axis=-1, keepdims=True)).astype(jnp.bfloat16)
    output = jnp.einsum(
        "rhk,kd->rhd", probs, cache_latent[:, :KVL], preferred_element_type=jnp.float32
    )
    output = jnp.where(alive[:, None, None], output, jnp.float32(0.0))
    return output.astype(jnp.bfloat16).reshape(row_total, HEADS * KVL)


def member(block, kind):
    return 2 * block + ((kind ^ block) & 1)


def device(group, x, y):
    shift = group % 2
    return group * X_RING * Y_RING + (x + shift) % X_RING * Y_RING + (y + shift) % Y_RING


def block_groups(groups):
    return [
        [device(g, member(bx, sx), member(by, sy)) for sx in range(2) for sy in range(2)]
        for g in range(groups)
        for bx in range(X_RING // 2)
        for by in range(Y_RING // 2)
    ]


def kind_groups(groups):
    return [
        [
            device(g, member(bx, sx), member(by, sy))
            for by in range(Y_RING // 2)
            for bx in range(X_RING // 2)
        ]
        for g in range(groups)
        for sx in range(2)
        for sy in range(2)
    ]


def row_order(index, shift):
    slot, block = index & 7, index >> 3
    sx, sy, bx, by = block >> 4, (block >> 3) & 1, block & 1, (block >> 1) & 3
    x, y = member(bx, sx), member(by, sy)
    return ((((x + shift) & 3) << 3) + ((y + shift) & 7)) * 8 + slot


def partial_kernel(tile, units_hbm, down_hbm, out_hbm, units, down, out, in_sems, out_sems):
    tiles = down.shape[0]
    unit_copy = pltpu.make_async_copy(units_hbm, units, in_sems.at[tiles])
    unit_copy.start()
    copies = [
        pltpu.make_async_copy(down_hbm.at[:, pl.ds(j * tile, tile)], down.at[j], in_sems.at[j])
        for j in range(tiles)
    ]
    for copy in copies:
        copy.start()
    total = units.shape[1]
    shift = lax.axis_index("dp") & 1
    order = row_order(lax.broadcasted_iota(jnp.int32, (total, total), 0), shift)
    pick = order == lax.broadcasted_iota(jnp.int32, (total, total), 1)
    pick = jnp.where(pick, 1.0, 0.0).astype(jnp.bfloat16)
    unit_copy.wait()
    ordered = lax.dot_general(
        pick, units[...], (((1,), (1,)), ((), ())), preferred_element_type=jnp.float32
    ).astype(jnp.bfloat16)
    sends = []
    for j, copy in enumerate(copies):
        copy.wait()
        out[j] = jnp.dot(ordered, down[j], preferred_element_type=jnp.float32).astype(jnp.bfloat16)
        send = pltpu.make_async_copy(out.at[j], out_hbm.at[:, pl.ds(j * tile, tile)], out_sems.at[j])
        send.start()
        sends.append(send)
    for send in sends:
        send.wait()


def partial_sums(units_t, down_proj):
    units, total = units_t.shape
    width = down_proj.shape[1]
    tiles = width // TILE
    return pl.pallas_call(
        functools.partial(partial_kernel, TILE),
        out_shape=jax.ShapeDtypeStruct((total, width), jnp.bfloat16),
        in_specs=[
            pl.BlockSpec(memory_space=pl.ANY),
            pl.BlockSpec(memory_space=pl.ANY),
        ],
        out_specs=pl.BlockSpec(memory_space=pl.ANY),
        scratch_shapes=[
            pltpu.VMEM((units, total), jnp.bfloat16),
            pltpu.VMEM((tiles, units, TILE), jnp.bfloat16),
            pltpu.VMEM((tiles, total, TILE), jnp.bfloat16),
            pltpu.SemaphoreType.DMA((tiles + 1,)),
            pltpu.SemaphoreType.DMA((tiles,)),
        ],
        compiler_params=pltpu.CompilerParams(vmem_limit_bytes=56 * 2**20),
        cost_estimate=pl.CostEstimate(
            flops=2 * total * units * width,
            bytes_accessed=2 * (units * (width + total) + total * width),
            transcendentals=0,
        ),
        name="partial_sums",
    )(units_t, down_proj)


def sum_kernel(parts, in_ref, out_ref):
    rows = out_ref.shape[0]
    value = in_ref[pl.ds(0, rows), :].astype(jnp.float32)
    for part in range(1, parts):
        value += in_ref[pl.ds(part * rows, rows), :].astype(jnp.float32)
    out_ref[...] = value.astype(jnp.bfloat16)


def sum_parts(values, parts):
    rows, width = values.shape[0] // parts, values.shape[1]
    return pl.pallas_call(
        functools.partial(sum_kernel, parts),
        out_shape=jax.ShapeDtypeStruct((rows, width), jnp.bfloat16),
        compiler_params=pltpu.CompilerParams(vmem_limit_bytes=16 * 2**20),
        cost_estimate=pl.CostEstimate(
            flops=values.size, bytes_accessed=2 * (values.size + rows * width), transcendentals=0
        ),
        name="sum_parts",
    )(values)


def final_kernel(count_ref, *refs):
    out_ref = refs[-1]
    rows = out_ref.shape[0]
    for (start, stop), ref in zip(zip(CUTS[:-1], CUTS[1:]), refs[:-1]):
        value = jnp.zeros((rows, stop - start), jnp.float32)
        for pair in range(0, ref.shape[0], 2 * rows):
            both = ref[pl.ds(pair, 2 * rows), :].astype(jnp.float32)
            value += both[:rows] + both[rows:]
        row = lax.broadcasted_iota(jnp.int32, value.shape, 0)
        value = jnp.where(row < count_ref[0], value, 0.0)
        out_ref[:, pl.ds(start, stop - start)] = value.astype(jnp.bfloat16)


def final_sum(counts, halves, rows):
    return pl.pallas_call(
        final_kernel,
        out_shape=jax.ShapeDtypeStruct((rows, CUTS[-1]), jnp.bfloat16),
        in_specs=[pl.BlockSpec(memory_space=pltpu.SMEM)]
        + [pl.BlockSpec(memory_space=pltpu.VMEM) for _ in halves],
        compiler_params=pltpu.CompilerParams(vmem_limit_bytes=16 * 2**20),
        name="final_sum",
    )(counts, *halves)


def exchange(values, groups):
    return lax.all_to_all(values, ("dp", "tp"), 0, 0, tiled=True, axis_index_groups=groups)


def solution(mesh):
    groups = mesh.shape["dp"]

    def shards(
        queries, cache_latent, row_counts, row_kinds, cache_lengths, positions, hidden_units, down_proj
    ):
        row_total = queries.shape[0]
        alive = lax.broadcasted_iota(jnp.int32, (row_total,), 0) < row_counts[0]
        part = partial_sums(hidden_units.T, down_proj)
        moved = exchange(part, block_groups(groups))
        attended = attend_local(queries, cache_latent, cache_lengths, positions, row_kinds, alive)
        moved, attended = lax.optimization_barrier((moved, attended))
        quarter = sum_parts(moved, 4)
        moved = exchange(quarter, kind_groups(groups))
        summed = final_sum(row_counts, [moved], row_total)
        return (attended, summed)

    placed = (
        P(("dp", "tp"), None),
        P(("dp", "tp"), None),
        P(("dp", "tp")),
        P(("dp", "tp")),
        P(("dp", "tp")),
        P(("dp", "tp")),
        P("dp", "tp"),
        P("tp", None),
    )
    return jax.shard_map(
        shards,
        mesh=mesh,
        in_specs=placed,
        out_specs=(P(("dp", "tp"), None), P(("dp", "tp"), None)),
        check_vma=False,
    )
```

```python
import functools

import jax
import jax.numpy as jnp
from jax import lax
from jax.experimental import pallas as pl
from jax.experimental.pallas import tpu as pltpu
from jax.sharding import PartitionSpec as P

HEADS = 64
KVL = 512
QK_DIM = 192
LAT = 576
X_RING = 4
Y_RING = 8
CUTS = (0, 3584)
TILE = 896


def attend_local(queries, cache_latent, lengths, offsets, kinds, alive):
    row_total = queries.shape[0]
    entries = cache_latent.shape[0]
    scale = QK_DIM ** (-0.5)
    query_rows = queries.reshape(row_total, HEADS, LAT)
    scores = (
        jnp.einsum("rhd,kd->rhk", query_rows, cache_latent, preferred_element_type=jnp.float32)
        * scale
    )
    index = lax.broadcasted_iota(jnp.int32, (1, entries), 1)
    top_entry = (lengths + offsets)[:, None]
    causal = index <= top_entry
    verify = (index < lengths[:, None]) | (index == top_entry)
    allowed = jnp.where(kinds[:, None] == 1, verify, causal)[:, None, :]
    masked = jnp.where(allowed, scores, jnp.float32(-1e30))
    peak = jnp.max(masked, axis=-1, keepdims=True)
    expo = jnp.where(allowed, jnp.exp(masked - peak), jnp.float32(0.0))
    probs = (expo / jnp.sum(expo, axis=-1, keepdims=True)).astype(jnp.bfloat16)
    output = jnp.einsum(
        "rhk,kd->rhd", probs, cache_latent[:, :KVL], preferred_element_type=jnp.float32
    )
    output = jnp.where(alive[:, None, None], output, jnp.float32(0.0))
    return output.astype(jnp.bfloat16).reshape(row_total, HEADS * KVL)


def member(block, kind):
    return 2 * block + ((kind ^ block) & 1)


def device(group, x, y):
    core = group % 2
    return group * X_RING * Y_RING + (x + (1 - core)) % X_RING * Y_RING + (y + (1 - core)) % Y_RING


def member_y(block, kind, core):
    flips = 6 + core * 0
    return 2 * block + (kind ^ ((flips >> block) & 1))


def block_groups(groups):
    return [
        [device(g, member(bx, sx), member_y(by, sy, g % 2)) for sx in range(2) for sy in range(2)]
        for g in range(groups)
        for bx in range(X_RING // 2)
        for by in range(Y_RING // 2)
    ]


def kind_groups(groups):
    return [
        [
            device(g, member(bx, sx), member_y(by, sy, g % 2))
            for by in range(Y_RING // 2)
            for bx in range(X_RING // 2)
        ]
        for g in range(groups)
        for sx in range(2)
        for sy in range(2)
    ]


def row_order(index, shift):
    slot, block = index & 7, index >> 3
    sx, sy, bx, by = block >> 4, (block >> 3) & 1, block & 1, (block >> 1) & 3
    x, y = member(bx, sx), member_y(by, sy, shift)
    return ((((x + (1 - shift)) & 3) << 3) + ((y + (1 - shift)) & 7)) * 8 + slot


def partial_kernel(tile, units_hbm, down_hbm, out_hbm, units, down, out, in_sems, out_sems):
    tiles = down.shape[0]
    unit_copy = pltpu.make_async_copy(units_hbm, units, in_sems.at[tiles])
    unit_copy.start()
    copies = [
        pltpu.make_async_copy(down_hbm.at[:, pl.ds(j * tile, tile)], down.at[j], in_sems.at[j])
        for j in range(tiles)
    ]
    for copy in copies:
        copy.start()
    total = units.shape[1]
    shift = lax.axis_index("dp") & 1
    order = row_order(lax.broadcasted_iota(jnp.int32, (total, total), 0), shift)
    pick = order == lax.broadcasted_iota(jnp.int32, (total, total), 1)
    pick = jnp.where(pick, 1.0, 0.0).astype(jnp.bfloat16)
    unit_copy.wait()
    ordered = lax.dot_general(
        pick, units[...], (((1,), (1,)), ((), ())), preferred_element_type=jnp.float32
    ).astype(jnp.bfloat16)
    sends = []
    for j, copy in enumerate(copies):
        copy.wait()
        out[j] = jnp.dot(ordered, down[j], preferred_element_type=jnp.float32).astype(jnp.bfloat16)
        send = pltpu.make_async_copy(out.at[j], out_hbm.at[:, pl.ds(j * tile, tile)], out_sems.at[j])
        send.start()
        sends.append(send)
    for send in sends:
        send.wait()


def partial_sums(units_t, down_proj):
    units, total = units_t.shape
    width = down_proj.shape[1]
    tiles = width // TILE
    return pl.pallas_call(
        functools.partial(partial_kernel, TILE),
        out_shape=jax.ShapeDtypeStruct((total, width), jnp.bfloat16),
        in_specs=[
            pl.BlockSpec(memory_space=pl.ANY),
            pl.BlockSpec(memory_space=pl.ANY),
        ],
        out_specs=pl.BlockSpec(memory_space=pl.ANY),
        scratch_shapes=[
            pltpu.VMEM((units, total), jnp.bfloat16),
            pltpu.VMEM((tiles, units, TILE), jnp.bfloat16),
            pltpu.VMEM((tiles, total, TILE), jnp.bfloat16),
            pltpu.SemaphoreType.DMA((tiles + 1,)),
            pltpu.SemaphoreType.DMA((tiles,)),
        ],
        compiler_params=pltpu.CompilerParams(vmem_limit_bytes=56 * 2**20),
        cost_estimate=pl.CostEstimate(
            flops=2 * total * units * width,
            bytes_accessed=2 * (units * (width + total) + total * width),
            transcendentals=0,
        ),
        name="partial_sums",
    )(units_t, down_proj)


def sum_kernel(parts, in_ref, out_ref):
    rows = out_ref.shape[0]
    value = in_ref[pl.ds(0, rows), :].astype(jnp.float32)
    for part in range(1, parts):
        value += in_ref[pl.ds(part * rows, rows), :].astype(jnp.float32)
    out_ref[...] = value.astype(jnp.bfloat16)


def sum_parts(values, parts):
    rows, width = values.shape[0] // parts, values.shape[1]
    return pl.pallas_call(
        functools.partial(sum_kernel, parts),
        out_shape=jax.ShapeDtypeStruct((rows, width), jnp.bfloat16),
        compiler_params=pltpu.CompilerParams(vmem_limit_bytes=16 * 2**20),
        cost_estimate=pl.CostEstimate(
            flops=values.size, bytes_accessed=2 * (values.size + rows * width), transcendentals=0
        ),
        name="sum_parts",
    )(values)


def final_kernel(count_ref, *refs):
    out_ref = refs[-1]
    rows = out_ref.shape[0]
    for (start, stop), ref in zip(zip(CUTS[:-1], CUTS[1:]), refs[:-1]):
        value = jnp.zeros((rows, stop - start), jnp.float32)
        for pair in range(0, ref.shape[0], 2 * rows):
            both = ref[pl.ds(pair, 2 * rows), :].astype(jnp.float32)
            value += both[:rows] + both[rows:]
        row = lax.broadcasted_iota(jnp.int32, value.shape, 0)
        value = jnp.where(row < count_ref[0], value, 0.0)
        out_ref[:, pl.ds(start, stop - start)] = value.astype(jnp.bfloat16)


def final_sum(counts, halves, rows):
    return pl.pallas_call(
        final_kernel,
        out_shape=jax.ShapeDtypeStruct((rows, CUTS[-1]), jnp.bfloat16),
        in_specs=[pl.BlockSpec(memory_space=pltpu.SMEM)]
        + [pl.BlockSpec(memory_space=pltpu.VMEM) for _ in halves],
        compiler_params=pltpu.CompilerParams(vmem_limit_bytes=16 * 2**20),
        name="final_sum",
    )(counts, *halves)


def exchange(values, groups):
    return lax.all_to_all(values, ("dp", "tp"), 0, 0, tiled=True, axis_index_groups=groups)


def solution(mesh):
    groups = mesh.shape["dp"]

    def shards(
        queries, cache_latent, row_counts, row_kinds, cache_lengths, positions, hidden_units, down_proj
    ):
        row_total = queries.shape[0]
        alive = lax.broadcasted_iota(jnp.int32, (row_total,), 0) < row_counts[0]
        part = partial_sums(hidden_units.T, down_proj)
        moved = exchange(part, block_groups(groups))
        attended = attend_local(queries, cache_latent, cache_lengths, positions, row_kinds, alive)
        moved, attended = lax.optimization_barrier((moved, attended))
        quarter = sum_parts(moved, 4)
        moved = exchange(quarter, kind_groups(groups))
        summed = final_sum(row_counts, [moved], row_total)
        return (attended, summed)

    placed = (
        P(("dp", "tp"), None),
        P(("dp", "tp"), None),
        P(("dp", "tp")),
        P(("dp", "tp")),
        P(("dp", "tp")),
        P(("dp", "tp")),
        P("dp", "tp"),
        P("tp", None),
    )
    return jax.shard_map(
        shards,
        mesh=mesh,
        in_specs=placed,
        out_specs=(P(("dp", "tp"), None), P(("dp", "tp"), None)),
        check_vma=False,
    )
```

```python
import functools

import jax
import jax.numpy as jnp
from jax import lax
from jax.experimental import pallas as pl
from jax.experimental.pallas import tpu as pltpu
from jax.sharding import PartitionSpec as P

HEADS = 64
KVL = 512
QK_DIM = 192
LAT = 576
X_RING = 4
Y_RING = 8
TILE = 1792


def attend_local(queries, cache_latent, lengths, offsets, kinds, alive):
    row_total = queries.shape[0]
    entries = cache_latent.shape[0]
    scale = QK_DIM ** (-0.5)
    query_rows = queries.reshape(row_total, HEADS, LAT)
    scores = (
        jnp.einsum("rhd,kd->rhk", query_rows, cache_latent, preferred_element_type=jnp.float32)
        * scale
    )
    index = lax.broadcasted_iota(jnp.int32, (1, entries), 1)
    top_entry = (lengths + offsets)[:, None]
    causal = index <= top_entry
    verify = (index < lengths[:, None]) | (index == top_entry)
    allowed = jnp.where(kinds[:, None] == 1, verify, causal)[:, None, :]
    masked = jnp.where(allowed, scores, jnp.float32(-1e30))
    peak = jnp.max(masked, axis=-1, keepdims=True)
    expo = jnp.where(allowed, jnp.exp(masked - peak), jnp.float32(0.0))
    probs = (expo / jnp.sum(expo, axis=-1, keepdims=True)).astype(jnp.bfloat16)
    output = jnp.einsum(
        "rhk,kd->rhd", probs, cache_latent[:, :KVL], preferred_element_type=jnp.float32
    )
    output = jnp.where(alive[:, None, None], output, jnp.float32(0.0))
    return output.astype(jnp.bfloat16).reshape(row_total, HEADS * KVL)


FLIPS = (6, 12)


def member(block, kind):
    return 2 * block + ((kind ^ block) & 1)


def member_y(block, kind, core):
    flips = FLIPS[0] + core * (FLIPS[1] - FLIPS[0])
    return 2 * block + (kind ^ ((flips >> block) & 1))


def device(group, x, y):
    shift = 1 - group % 2
    return group * X_RING * Y_RING + (x + shift) % X_RING * Y_RING + (y + shift) % Y_RING


def flip_pairs(groups, flip):
    return [
        (device(g, x, y), device(g, x ^ (flip >> 1), y ^ (flip & 1)))
        for g in range(groups)
        for x in range(X_RING)
        for y in range(Y_RING)
    ]


def kind_groups(groups):
    return [
        [
            device(g, member(bx, sx), member_y(by, sy, g % 2))
            for by in range(Y_RING // 2)
            for bx in range(X_RING // 2)
        ]
        for g in range(groups)
        for sx in range(2)
        for sy in range(2)
    ]


def own_kind(core, place):
    shift = 1 - core
    x, y = ((place >> 3) - shift) & 3, (place - shift) & 7
    flips = FLIPS[0] + core * (FLIPS[1] - FLIPS[0])
    return 2 * ((x ^ (x >> 1)) & 1) + ((y ^ (flips >> (y >> 1))) & 1)


def row_order(index, core, kind):
    slot, block = index & 7, index >> 3
    to = (block >> 3) ^ kind
    sx, sy, by, bx = to >> 1, to & 1, (block >> 1) & 3, block & 1
    x, y, shift = member(bx, sx), member_y(by, sy, core), 1 - core
    return ((((x + shift) & 3) << 3) + ((y + shift) & 7)) * 8 + slot


def partial_kernel(tile, units_hbm, down_hbm, *refs):
    (units, down, out, in_sems, out_sems), outs_hbm = refs[-5:], refs[:-5]
    rows = outs_hbm[0].shape[0]
    tiles = down.shape[0]
    unit_copy = pltpu.make_async_copy(units_hbm, units, in_sems.at[tiles])
    unit_copy.start()
    copies = [
        pltpu.make_async_copy(down_hbm.at[:, pl.ds(j * tile, tile)], down.at[j], in_sems.at[j])
        for j in range(tiles)
    ]
    for copy in copies:
        copy.start()
    total = units.shape[1]
    core = lax.axis_index("dp") & 1
    kind = own_kind(core, lax.axis_index("tp"))
    order = row_order(lax.broadcasted_iota(jnp.int32, (total, total), 0), core, kind)
    pick = order == lax.broadcasted_iota(jnp.int32, (total, total), 1)
    pick = jnp.where(pick, 1.0, 0.0).astype(jnp.bfloat16)
    unit_copy.wait()
    ordered = lax.dot_general(
        pick, units[...], (((1,), (1,)), ((), ())), preferred_element_type=jnp.float32
    ).astype(jnp.bfloat16)
    sends = []
    for j, copy in enumerate(copies):
        copy.wait()
        out[j] = jnp.dot(ordered, down[j], preferred_element_type=jnp.float32).astype(jnp.bfloat16)
        for k, out_hbm in enumerate(outs_hbm):
            send = pltpu.make_async_copy(
                out.at[j, pl.ds(k * rows, rows)],
                out_hbm.at[:, pl.ds(j * tile, tile)],
                out_sems.at[j, k],
            )
            send.start()
            sends.append(send)
    for send in sends:
        send.wait()


def partial_sums(units_t, down_proj):
    units, total = units_t.shape
    width = down_proj.shape[1]
    tiles = width // TILE
    return pl.pallas_call(
        functools.partial(partial_kernel, TILE),
        out_shape=[jax.ShapeDtypeStruct((total // 4, width), jnp.bfloat16)] * 4,
        in_specs=[
            pl.BlockSpec(memory_space=pl.ANY),
            pl.BlockSpec(memory_space=pl.ANY),
        ],
        out_specs=[pl.BlockSpec(memory_space=pl.ANY)] * 4,
        scratch_shapes=[
            pltpu.VMEM((units, total), jnp.bfloat16),
            pltpu.VMEM((tiles, units, TILE), jnp.bfloat16),
            pltpu.VMEM((tiles, total, TILE), jnp.bfloat16),
            pltpu.SemaphoreType.DMA((tiles + 1,)),
            pltpu.SemaphoreType.DMA((tiles, 4)),
        ],
        compiler_params=pltpu.CompilerParams(vmem_limit_bytes=56 * 2**20),
        cost_estimate=pl.CostEstimate(
            flops=2 * total * units * width,
            bytes_accessed=2 * (units * (width + total) + total * width),
            transcendentals=0,
        ),
        name="partial_sums",
    )(units_t, down_proj)


def sum_kernel(*refs):
    value = refs[0][...].astype(jnp.float32)
    for ref in refs[1:-1]:
        value += ref[...].astype(jnp.float32)
    refs[-1][...] = value.astype(jnp.bfloat16)


def sum_arrays(*arrays):
    return pl.pallas_call(
        sum_kernel,
        out_shape=jax.ShapeDtypeStruct(arrays[0].shape, jnp.bfloat16),
        compiler_params=pltpu.CompilerParams(vmem_limit_bytes=16 * 2**20),
        name="sum_arrays",
    )(*arrays)


def final_kernel(count_ref, in_ref, out_ref):
    rows = out_ref.shape[0]
    value = jnp.zeros(out_ref.shape, jnp.float32)
    for pair in range(0, in_ref.shape[0], 2 * rows):
        both = in_ref[pl.ds(pair, 2 * rows), :].astype(jnp.float32)
        value += both[:rows] + both[rows:]
    row = lax.broadcasted_iota(jnp.int32, value.shape, 0)
    out_ref[...] = jnp.where(row < count_ref[0], value, 0.0).astype(jnp.bfloat16)


def final_sum(counts, values, rows):
    return pl.pallas_call(
        final_kernel,
        out_shape=jax.ShapeDtypeStruct((rows, values.shape[1]), jnp.bfloat16),
        in_specs=[
            pl.BlockSpec(memory_space=pltpu.SMEM),
            pl.BlockSpec(memory_space=pltpu.VMEM),
        ],
        compiler_params=pltpu.CompilerParams(vmem_limit_bytes=16 * 2**20),
        name="final_sum",
    )(counts, values)


def exchange(values, groups):
    return lax.all_to_all(values, ("dp", "tp"), 0, 0, tiled=True, axis_index_groups=groups)


def solution(mesh):
    groups = mesh.shape["dp"]

    def shards(
        queries, cache_latent, row_counts, row_kinds, cache_lengths, positions, hidden_units, down_proj
    ):
        row_total = queries.shape[0]
        alive = lax.broadcasted_iota(jnp.int32, (row_total,), 0) < row_counts[0]
        parts = list(partial_sums(hidden_units.T, down_proj))
        for flip in (3, 2, 1):
            parts[flip] = lax.ppermute(parts[flip], ("dp", "tp"), flip_pairs(groups, flip))
        attended = attend_local(queries, cache_latent, cache_lengths, positions, row_kinds, alive)
        quarter = sum_arrays(*(parts[flip] for flip in (0, 3, 2, 1)))
        quarter, attended = lax.optimization_barrier((quarter, attended))
        moved = exchange(quarter, kind_groups(groups))
        summed = final_sum(row_counts, moved, row_total)
        return (attended, summed)

    placed = (
        P(("dp", "tp"), None),
        P(("dp", "tp"), None),
        P(("dp", "tp")),
        P(("dp", "tp")),
        P(("dp", "tp")),
        P(("dp", "tp")),
        P("dp", "tp"),
        P("tp", None),
    )
    return jax.shard_map(
        shards,
        mesh=mesh,
        in_specs=placed,
        out_specs=(P(("dp", "tp"), None), P(("dp", "tp"), None)),
        check_vma=False,
    )
```

```python
import functools

import jax
import jax.numpy as jnp
from jax import lax
from jax.experimental import pallas as pl
from jax.experimental.pallas import tpu as pltpu
from jax.sharding import PartitionSpec as P

HEADS = 64
KVL = 512
QK_DIM = 192
LAT = 576
X_RING = 4
Y_RING = 8
TILE = 1792


def attend_local(queries, cache_latent, lengths, offsets, kinds, alive):
    row_total = queries.shape[0]
    entries = cache_latent.shape[0]
    scale = QK_DIM ** (-0.5)
    query_rows = queries.reshape(row_total, HEADS, LAT)
    scores = (
        jnp.einsum("rhd,kd->rhk", query_rows, cache_latent, preferred_element_type=jnp.float32)
        * scale
    )
    index = lax.broadcasted_iota(jnp.int32, (1, entries), 1)
    top_entry = (lengths + offsets)[:, None]
    causal = index <= top_entry
    verify = (index < lengths[:, None]) | (index == top_entry)
    allowed = jnp.where(kinds[:, None] == 1, verify, causal)[:, None, :]
    masked = jnp.where(allowed, scores, jnp.float32(-1e30))
    peak = jnp.max(masked, axis=-1, keepdims=True)
    expo = jnp.where(allowed, jnp.exp(masked - peak), jnp.float32(0.0))
    probs = (expo / jnp.sum(expo, axis=-1, keepdims=True)).astype(jnp.bfloat16)
    output = jnp.einsum(
        "rhk,kd->rhd", probs, cache_latent[:, :KVL], preferred_element_type=jnp.float32
    )
    output = jnp.where(alive[:, None, None], output, jnp.float32(0.0))
    return output.astype(jnp.bfloat16).reshape(row_total, HEADS * KVL)


FLIPS = 6


def member(block, kind):
    return 2 * block + ((kind ^ block) & 1)


def member_y(block, kind):
    return 2 * block + (kind ^ ((FLIPS >> block) & 1))


def device(group, x, y):
    shift = 1 - group % 2
    return group * X_RING * Y_RING + (x + shift) % X_RING * Y_RING + (y + shift) % Y_RING


def flip_pairs(groups, flip):
    return [
        (device(g, x, y), device(g, x ^ (flip >> 1), y ^ (flip & 1)))
        for g in range(groups)
        for x in range(X_RING)
        for y in range(Y_RING)
    ]


def kind_groups(groups):
    return [
        [
            device(g, member(bx, sx), member_y(by, sy))
            for by in range(Y_RING // 2)
            for bx in range(X_RING // 2)
        ]
        for g in range(groups)
        for sx in range(2)
        for sy in range(2)
    ]


def own_kind(core, place):
    shift = 1 - core
    x, y = ((place >> 3) - shift) & 3, (place - shift) & 7
    return 2 * ((x ^ (x >> 1)) & 1) + ((y ^ (FLIPS >> (y >> 1))) & 1)


def row_order(index, core, kind):
    slot, block = index & 7, index >> 3
    to = (block >> 3) ^ kind
    sx, sy, by, bx = to >> 1, to & 1, (block >> 1) & 3, block & 1
    x, y, shift = member(bx, sx), member_y(by, sy), 1 - core
    return ((((x + shift) & 3) << 3) + ((y + shift) & 7)) * 8 + slot


def partial_kernel(tile, units_hbm, down_hbm, *refs):
    (units, down, out, in_sems, out_sems), outs_hbm = refs[-5:], refs[:-5]
    rows = outs_hbm[0].shape[0]
    tiles = down.shape[0]
    unit_copy = pltpu.make_async_copy(units_hbm, units, in_sems.at[tiles])
    unit_copy.start()
    copies = [
        pltpu.make_async_copy(down_hbm.at[:, pl.ds(j * tile, tile)], down.at[j], in_sems.at[j])
        for j in range(tiles)
    ]
    for copy in copies:
        copy.start()
    total = units.shape[1]
    core = lax.axis_index("dp") & 1
    kind = own_kind(core, lax.axis_index("tp"))
    order = row_order(lax.broadcasted_iota(jnp.int32, (total, total), 0), core, kind)
    pick = order == lax.broadcasted_iota(jnp.int32, (total, total), 1)
    pick = jnp.where(pick, 1.0, 0.0).astype(jnp.bfloat16)
    unit_copy.wait()
    ordered = lax.dot_general(
        pick, units[...], (((1,), (1,)), ((), ())), preferred_element_type=jnp.float32
    ).astype(jnp.bfloat16)
    sends = []
    for j, copy in enumerate(copies):
        copy.wait()
        out[j] = jnp.dot(ordered, down[j], preferred_element_type=jnp.float32).astype(jnp.bfloat16)
        for k, out_hbm in enumerate(outs_hbm):
            send = pltpu.make_async_copy(
                out.at[j, pl.ds(k * rows, rows)],
                out_hbm.at[:, pl.ds(j * tile, tile)],
                out_sems.at[j, k],
            )
            send.start()
            sends.append(send)
    for send in sends:
        send.wait()


def partial_sums(units_t, down_proj):
    units, total = units_t.shape
    width = down_proj.shape[1]
    tiles = width // TILE
    return pl.pallas_call(
        functools.partial(partial_kernel, TILE),
        out_shape=[jax.ShapeDtypeStruct((total // 4, width), jnp.bfloat16)] * 4,
        in_specs=[
            pl.BlockSpec(memory_space=pl.ANY),
            pl.BlockSpec(memory_space=pl.ANY),
        ],
        out_specs=[pl.BlockSpec(memory_space=pl.ANY)] * 4,
        scratch_shapes=[
            pltpu.VMEM((units, total), jnp.bfloat16),
            pltpu.VMEM((tiles, units, TILE), jnp.bfloat16),
            pltpu.VMEM((tiles, total, TILE), jnp.bfloat16),
            pltpu.SemaphoreType.DMA((tiles + 1,)),
            pltpu.SemaphoreType.DMA((tiles, 4)),
        ],
        compiler_params=pltpu.CompilerParams(vmem_limit_bytes=56 * 2**20),
        cost_estimate=pl.CostEstimate(
            flops=2 * total * units * width,
            bytes_accessed=2 * (units * (width + total) + total * width),
            transcendentals=0,
        ),
        name="partial_sums",
    )(units_t, down_proj)


def sum_kernel(*refs):
    value = refs[0][...].astype(jnp.float32)
    for ref in refs[1:-1]:
        value += ref[...].astype(jnp.float32)
    refs[-1][...] = value.astype(jnp.bfloat16)


def sum_arrays(*arrays):
    return pl.pallas_call(
        sum_kernel,
        out_shape=jax.ShapeDtypeStruct(arrays[0].shape, jnp.bfloat16),
        compiler_params=pltpu.CompilerParams(vmem_limit_bytes=16 * 2**20),
        name="sum_arrays",
    )(*arrays)


def final_kernel(count_ref, in_ref, out_ref):
    rows = out_ref.shape[0]
    value = jnp.zeros(out_ref.shape, jnp.float32)
    for pair in range(0, in_ref.shape[0], 2 * rows):
        both = in_ref[pl.ds(pair, 2 * rows), :].astype(jnp.float32)
        value += both[:rows] + both[rows:]
    row = lax.broadcasted_iota(jnp.int32, value.shape, 0)
    out_ref[...] = jnp.where(row < count_ref[0], value, 0.0).astype(jnp.bfloat16)


def final_sum(counts, values, rows):
    return pl.pallas_call(
        final_kernel,
        out_shape=jax.ShapeDtypeStruct((rows, values.shape[1]), jnp.bfloat16),
        in_specs=[
            pl.BlockSpec(memory_space=pltpu.SMEM),
            pl.BlockSpec(memory_space=pltpu.VMEM),
        ],
        compiler_params=pltpu.CompilerParams(vmem_limit_bytes=16 * 2**20),
        name="final_sum",
    )(counts, values)


def exchange(values, groups):
    return lax.all_to_all(values, ("dp", "tp"), 0, 0, tiled=True, axis_index_groups=groups)


def solution(mesh):
    groups = mesh.shape["dp"]

    def shards(
        queries, cache_latent, row_counts, row_kinds, cache_lengths, positions, hidden_units, down_proj
    ):
        row_total = queries.shape[0]
        alive = lax.broadcasted_iota(jnp.int32, (row_total,), 0) < row_counts[0]
        parts = list(partial_sums(hidden_units.T, down_proj))
        for flip in (3, 2, 1):
            parts[flip] = lax.ppermute(parts[flip], ("dp", "tp"), flip_pairs(groups, flip))
        attended = attend_local(queries, cache_latent, cache_lengths, positions, row_kinds, alive)
        quarter = sum_arrays(*(parts[flip] for flip in (0, 3, 2, 1)))
        quarter, attended = lax.optimization_barrier((quarter, attended))
        moved = exchange(quarter, kind_groups(groups))
        summed = final_sum(row_counts, moved, row_total)
        return (attended, summed)

    placed = (
        P(("dp", "tp"), None),
        P(("dp", "tp"), None),
        P(("dp", "tp")),
        P(("dp", "tp")),
        P(("dp", "tp")),
        P(("dp", "tp")),
        P("dp", "tp"),
        P("tp", None),
    )
    return jax.shard_map(
        shards,
        mesh=mesh,
        in_specs=placed,
        out_specs=(P(("dp", "tp"), None), P(("dp", "tp"), None)),
        check_vma=False,
    )
```

```python
import functools

import jax
import jax.numpy as jnp
from jax import lax
from jax.experimental import pallas as pl
from jax.experimental.pallas import tpu as pltpu
from jax.sharding import PartitionSpec as P

HEADS = 64
KVL = 512
QK_DIM = 192
LAT = 576
X_RING = 4
Y_RING = 8
TILE = 1792


def attend_local(queries, cache_latent, lengths, offsets, kinds, alive):
    row_total = queries.shape[0]
    entries = cache_latent.shape[0]
    scale = QK_DIM ** (-0.5)
    query_rows = queries.reshape(row_total, HEADS, LAT)
    scores = (
        jnp.einsum("rhd,kd->rhk", query_rows, cache_latent, preferred_element_type=jnp.float32)
        * scale
    )
    index = lax.broadcasted_iota(jnp.int32, (1, entries), 1)
    top_entry = (lengths + offsets)[:, None]
    causal = index <= top_entry
    verify = (index < lengths[:, None]) | (index == top_entry)
    allowed = jnp.where(kinds[:, None] == 1, verify, causal)[:, None, :]
    masked = jnp.where(allowed, scores, jnp.float32(-1e30))
    peak = jnp.max(masked, axis=-1, keepdims=True)
    expo = jnp.where(allowed, jnp.exp(masked - peak), jnp.float32(0.0))
    probs = (expo / jnp.sum(expo, axis=-1, keepdims=True)).astype(jnp.bfloat16)
    output = jnp.einsum(
        "rhk,kd->rhd", probs, cache_latent[:, :KVL], preferred_element_type=jnp.float32
    )
    output = jnp.where(alive[:, None, None], output, jnp.float32(0.0))
    return output.astype(jnp.bfloat16).reshape(row_total, HEADS * KVL)


FLIPS = 6


def member(block, kind):
    return 2 * block + ((kind ^ block) & 1)


def member_y(block, kind):
    return 2 * block + (kind ^ ((FLIPS >> block) & 1))


def device(group, x, y):
    shift = 1 - group % 2
    return group * X_RING * Y_RING + (x + shift) % X_RING * Y_RING + (y + shift) % Y_RING


def flip_pairs(groups, flip):
    return [
        (device(g, x, y), device(g, x ^ (flip >> 1), y ^ (flip & 1)))
        for g in range(groups)
        for x in range(X_RING)
        for y in range(Y_RING)
    ]


def kind_groups(groups):
    return [
        [
            device(g, member(bx, sx), member_y(by, sy))
            for by, bx in ((0, 0), (0, 1), (1, 1), (1, 0), (2, 0), (2, 1), (3, 1), (3, 0))
        ]
        for g in range(groups)
        for sx in range(2)
        for sy in range(2)
    ]


def own_kind(core, place):
    shift = 1 - core
    x, y = ((place >> 3) - shift) & 3, (place - shift) & 7
    return 2 * ((x ^ (x >> 1)) & 1) + ((y ^ (FLIPS >> (y >> 1))) & 1)


def row_order(index, core, kind):
    slot, block = index & 7, index >> 3
    to = (block >> 3) ^ kind
    sx, sy, by, bx = to >> 1, to & 1, (64080 >> (2 * (block & 7))) & 3, (102 >> (block & 7)) & 1
    x, y, shift = member(bx, sx), member_y(by, sy), 1 - core
    return ((((x + shift) & 3) << 3) + ((y + shift) & 7)) * 8 + slot


def partial_kernel(tile, units_hbm, down_hbm, *refs):
    (units, down, out, in_sems, out_sems), outs_hbm = refs[-5:], refs[:-5]
    rows = outs_hbm[0].shape[0]
    tiles = down.shape[0]
    unit_copy = pltpu.make_async_copy(units_hbm, units, in_sems.at[tiles])
    unit_copy.start()
    copies = [
        pltpu.make_async_copy(down_hbm.at[:, pl.ds(j * tile, tile)], down.at[j], in_sems.at[j])
        for j in range(tiles)
    ]
    for copy in copies:
        copy.start()
    total = units.shape[1]
    core = lax.axis_index("dp") & 1
    kind = own_kind(core, lax.axis_index("tp"))
    order = row_order(lax.broadcasted_iota(jnp.int32, (total, total), 0), core, kind)
    pick = order == lax.broadcasted_iota(jnp.int32, (total, total), 1)
    pick = jnp.where(pick, 1.0, 0.0).astype(jnp.bfloat16)
    unit_copy.wait()
    ordered = lax.dot_general(
        pick, units[...], (((1,), (1,)), ((), ())), preferred_element_type=jnp.float32
    ).astype(jnp.bfloat16)
    sends = []
    for j, copy in enumerate(copies):
        copy.wait()
        out[j] = jnp.dot(ordered, down[j], preferred_element_type=jnp.float32).astype(jnp.bfloat16)
        for k, out_hbm in enumerate(outs_hbm):
            send = pltpu.make_async_copy(
                out.at[j, pl.ds(k * rows, rows)],
                out_hbm.at[:, pl.ds(j * tile, tile)],
                out_sems.at[j, k],
            )
            send.start()
            sends.append(send)
    for send in sends:
        send.wait()


def partial_sums(units_t, down_proj):
    units, total = units_t.shape
    width = down_proj.shape[1]
    tiles = width // TILE
    return pl.pallas_call(
        functools.partial(partial_kernel, TILE),
        out_shape=[jax.ShapeDtypeStruct((total // 4, width), jnp.bfloat16)] * 4,
        in_specs=[
            pl.BlockSpec(memory_space=pl.ANY),
            pl.BlockSpec(memory_space=pl.ANY),
        ],
        out_specs=[pl.BlockSpec(memory_space=pl.ANY)] * 4,
        scratch_shapes=[
            pltpu.VMEM((units, total), jnp.bfloat16),
            pltpu.VMEM((tiles, units, TILE), jnp.bfloat16),
            pltpu.VMEM((tiles, total, TILE), jnp.bfloat16),
            pltpu.SemaphoreType.DMA((tiles + 1,)),
            pltpu.SemaphoreType.DMA((tiles, 4)),
        ],
        compiler_params=pltpu.CompilerParams(vmem_limit_bytes=56 * 2**20),
        cost_estimate=pl.CostEstimate(
            flops=2 * total * units * width,
            bytes_accessed=2 * (units * (width + total) + total * width),
            transcendentals=0,
        ),
        name="partial_sums",
    )(units_t, down_proj)


def sum_kernel(*refs):
    value = refs[0][...].astype(jnp.float32)
    for ref in refs[1:-1]:
        value += ref[...].astype(jnp.float32)
    refs[-1][...] = value.astype(jnp.bfloat16)


def sum_arrays(*arrays):
    return pl.pallas_call(
        sum_kernel,
        out_shape=jax.ShapeDtypeStruct(arrays[0].shape, jnp.bfloat16),
        compiler_params=pltpu.CompilerParams(vmem_limit_bytes=16 * 2**20),
        name="sum_arrays",
    )(*arrays)


def final_kernel(count_ref, in_ref, out_ref):
    rows = out_ref.shape[0]
    value = jnp.zeros(out_ref.shape, jnp.float32)
    for pair in range(0, in_ref.shape[0], 2 * rows):
        both = in_ref[pl.ds(pair, 2 * rows), :].astype(jnp.float32)
        value += both[:rows] + both[rows:]
    row = lax.broadcasted_iota(jnp.int32, value.shape, 0)
    out_ref[...] = jnp.where(row < count_ref[0], value, 0.0).astype(jnp.bfloat16)


def final_sum(counts, values, rows):
    return pl.pallas_call(
        final_kernel,
        out_shape=jax.ShapeDtypeStruct((rows, values.shape[1]), jnp.bfloat16),
        in_specs=[
            pl.BlockSpec(memory_space=pltpu.SMEM),
            pl.BlockSpec(memory_space=pltpu.VMEM),
        ],
        compiler_params=pltpu.CompilerParams(vmem_limit_bytes=16 * 2**20),
        name="final_sum",
    )(counts, values)


def exchange(values, groups):
    return lax.all_to_all(values, ("dp", "tp"), 0, 0, tiled=True, axis_index_groups=groups)


def solution(mesh):
    groups = mesh.shape["dp"]

    def shards(
        queries, cache_latent, row_counts, row_kinds, cache_lengths, positions, hidden_units, down_proj
    ):
        row_total = queries.shape[0]
        alive = lax.broadcasted_iota(jnp.int32, (row_total,), 0) < row_counts[0]
        parts = list(partial_sums(hidden_units.T, down_proj))
        for flip in (3, 2, 1):
            parts[flip] = lax.ppermute(parts[flip], ("dp", "tp"), flip_pairs(groups, flip))
        attended = attend_local(queries, cache_latent, cache_lengths, positions, row_kinds, alive)
        quarter = sum_arrays(*(parts[flip] for flip in (0, 3, 2, 1)))
        quarter, attended = lax.optimization_barrier((quarter, attended))
        moved = exchange(quarter, kind_groups(groups))
        summed = final_sum(row_counts, moved, row_total)
        return (attended, summed)

    placed = (
        P(("dp", "tp"), None),
        P(("dp", "tp"), None),
        P(("dp", "tp")),
        P(("dp", "tp")),
        P(("dp", "tp")),
        P(("dp", "tp")),
        P("dp", "tp"),
        P("tp", None),
    )
    return jax.shard_map(
        shards,
        mesh=mesh,
        in_specs=placed,
        out_specs=(P(("dp", "tp"), None), P(("dp", "tp"), None)),
        check_vma=False,
    )
```

```python
import functools

import jax
import jax.numpy as jnp
from jax import lax
from jax.experimental import pallas as pl
from jax.experimental.pallas import tpu as pltpu
from jax.sharding import PartitionSpec as P

HEADS = 64
KVL = 512
QK_DIM = 192
LAT = 576
X_RING = 4
Y_RING = 8
TILE = 1792


def attend_local(queries, cache_latent, lengths, offsets, kinds, alive):
    row_total = queries.shape[0]
    entries = cache_latent.shape[0]
    scale = QK_DIM ** (-0.5)
    query_rows = queries.reshape(row_total, HEADS, LAT)
    scores = (
        jnp.einsum("rhd,kd->rhk", query_rows, cache_latent, preferred_element_type=jnp.float32)
        * scale
    )
    index = lax.broadcasted_iota(jnp.int32, (1, entries), 1)
    top_entry = (lengths + offsets)[:, None]
    causal = index <= top_entry
    verify = (index < lengths[:, None]) | (index == top_entry)
    allowed = jnp.where(kinds[:, None] == 1, verify, causal)[:, None, :]
    masked = jnp.where(allowed, scores, jnp.float32(-1e30))
    peak = jnp.max(masked, axis=-1, keepdims=True)
    expo = jnp.where(allowed, jnp.exp(masked - peak), jnp.float32(0.0))
    probs = (expo / jnp.sum(expo, axis=-1, keepdims=True)).astype(jnp.bfloat16)
    output = jnp.einsum(
        "rhk,kd->rhd", probs, cache_latent[:, :KVL], preferred_element_type=jnp.float32
    )
    output = jnp.where(alive[:, None, None], output, jnp.float32(0.0))
    return output.astype(jnp.bfloat16).reshape(row_total, HEADS * KVL)


FLIPS = 6


def member(block, kind):
    return 2 * block + ((kind ^ block) & 1)


def member_y(block, kind):
    return 2 * block + (kind ^ ((FLIPS >> block) & 1))


def device(group, x, y):
    shift = 1 - group % 2
    return group * X_RING * Y_RING + (x + shift) % X_RING * Y_RING + (y + shift) % Y_RING


def flip_pairs(groups, flip):
    return [
        (device(g, x, y), device(g, x ^ (flip >> 1), y ^ (flip & 1)))
        for g in range(groups)
        for x in range(X_RING)
        for y in range(Y_RING)
    ]


def kind_groups(groups):
    return [
        [
            device(g, member(bx, sx), member_y(by, sy))
            for by, bx in ((0, 0), (0, 1), (1, 1), (1, 0), (2, 0), (2, 1), (3, 1), (3, 0))
        ]
        for g in range(groups)
        for sx in range(2)
        for sy in range(2)
    ]


def own_kind(core, place):
    shift = 1 - core
    x, y = ((place >> 3) - shift) & 3, (place - shift) & 7
    return 2 * ((x ^ (x >> 1)) & 1) + ((y ^ (FLIPS >> (y >> 1))) & 1)


def row_order(index, core, kind):
    slot, block = index & 7, index >> 3
    to = (block >> 3) ^ kind
    sx, sy, by, bx = to >> 1, to & 1, (64080 >> (2 * (block & 7))) & 3, (102 >> (block & 7)) & 1
    x, y, shift = member(bx, sx), member_y(by, sy), 1 - core
    return ((((x + shift) & 3) << 3) + ((y + shift) & 7)) * 8 + slot


def partial_kernel(tile, units_hbm, down_hbm, *refs):
    (units, down, out, in_sems, out_sems), outs_hbm = refs[-5:], refs[:-5]
    rows = outs_hbm[0].shape[0]
    tiles = down.shape[0]
    unit_copy = pltpu.make_async_copy(units_hbm, units, in_sems.at[tiles])
    unit_copy.start()
    copies = [
        pltpu.make_async_copy(down_hbm.at[:, pl.ds(j * tile, tile)], down.at[j], in_sems.at[j])
        for j in range(tiles)
    ]
    for copy in copies:
        copy.start()
    total = units.shape[1]
    core = lax.axis_index("dp") & 1
    kind = own_kind(core, lax.axis_index("tp"))
    order = row_order(lax.broadcasted_iota(jnp.int32, (total, total), 0), core, kind)
    pick = order == lax.broadcasted_iota(jnp.int32, (total, total), 1)
    pick = jnp.where(pick, 1.0, 0.0).astype(jnp.bfloat16)
    unit_copy.wait()
    ordered = lax.dot_general(
        pick, units[...], (((1,), (1,)), ((), ())), preferred_element_type=jnp.float32
    ).astype(jnp.bfloat16)
    sends = []
    for j, copy in enumerate(copies):
        copy.wait()
        out[j] = jnp.dot(ordered, down[j], preferred_element_type=jnp.float32).astype(jnp.bfloat16)
        for k, out_hbm in enumerate(outs_hbm):
            send = pltpu.make_async_copy(
                out.at[j, pl.ds(k * rows, rows)],
                out_hbm.at[:, pl.ds(j * tile, tile)],
                out_sems.at[j, k],
            )
            send.start()
            sends.append(send)
    for send in sends:
        send.wait()


def partial_sums(units_t, down_proj):
    units, total = units_t.shape
    width = down_proj.shape[1]
    tiles = width // TILE
    return pl.pallas_call(
        functools.partial(partial_kernel, TILE),
        out_shape=[jax.ShapeDtypeStruct((total // 4, width), jnp.bfloat16)] * 4,
        in_specs=[
            pl.BlockSpec(memory_space=pl.ANY),
            pl.BlockSpec(memory_space=pl.ANY),
        ],
        out_specs=[pl.BlockSpec(memory_space=pl.ANY)] * 4,
        scratch_shapes=[
            pltpu.VMEM((units, total), jnp.bfloat16),
            pltpu.VMEM((tiles, units, TILE), jnp.bfloat16),
            pltpu.VMEM((tiles, total, TILE), jnp.bfloat16),
            pltpu.SemaphoreType.DMA((tiles + 1,)),
            pltpu.SemaphoreType.DMA((tiles, 4)),
        ],
        compiler_params=pltpu.CompilerParams(vmem_limit_bytes=56 * 2**20),
        cost_estimate=pl.CostEstimate(
            flops=2 * total * units * width,
            bytes_accessed=2 * (units * (width + total) + total * width),
            transcendentals=0,
        ),
        name="partial_sums",
    )(units_t, down_proj)


def sum_kernel(*refs):
    value = refs[0][...].astype(jnp.float32)
    for ref in refs[1:-1]:
        value += ref[...].astype(jnp.float32)
    refs[-1][...] = value.astype(jnp.bfloat16)


def sum_arrays(*arrays):
    return pl.pallas_call(
        sum_kernel,
        out_shape=jax.ShapeDtypeStruct(arrays[0].shape, jnp.bfloat16),
        compiler_params=pltpu.CompilerParams(vmem_limit_bytes=16 * 2**20),
        name="sum_arrays",
    )(*arrays)


def final_kernel(count_ref, in_ref, out_ref):
    rows = out_ref.shape[0]
    value = jnp.zeros(out_ref.shape, jnp.float32)
    for pair in range(0, in_ref.shape[0], 2 * rows):
        both = in_ref[pl.ds(pair, 2 * rows), :].astype(jnp.float32)
        value += both[:rows] + both[rows:]
    row = lax.broadcasted_iota(jnp.int32, value.shape, 0)
    out_ref[...] = jnp.where(row < count_ref[0], value, 0.0).astype(jnp.bfloat16)


def final_sum(counts, values, rows):
    return pl.pallas_call(
        final_kernel,
        out_shape=jax.ShapeDtypeStruct((rows, values.shape[1]), jnp.bfloat16),
        in_specs=[
            pl.BlockSpec(memory_space=pltpu.SMEM),
            pl.BlockSpec(memory_space=pltpu.VMEM),
        ],
        compiler_params=pltpu.CompilerParams(vmem_limit_bytes=16 * 2**20),
        name="final_sum",
    )(counts, values)


def exchange(values, groups):
    return lax.all_to_all(values, ("dp", "tp"), 0, 0, tiled=True, axis_index_groups=groups)


def solution(mesh):
    groups = mesh.shape["dp"]

    def shards(
        queries, cache_latent, row_counts, row_kinds, cache_lengths, positions, hidden_units, down_proj
    ):
        row_total = queries.shape[0]
        alive = lax.broadcasted_iota(jnp.int32, (row_total,), 0) < row_counts[0]
        parts = list(partial_sums(hidden_units.T, down_proj))
        for flip in (3, 2, 1):
            parts[flip] = lax.ppermute(parts[flip], ("dp", "tp"), flip_pairs(groups, flip))
        attended = attend_local(queries, cache_latent, cache_lengths, positions, row_kinds, alive)
        quarter = sum_arrays(*(parts[flip] for flip in (0, 3, 1, 2)))
        quarter, attended = lax.optimization_barrier((quarter, attended))
        moved = exchange(quarter, kind_groups(groups))
        summed = final_sum(row_counts, moved, row_total)
        return (attended, summed)

    placed = (
        P(("dp", "tp"), None),
        P(("dp", "tp"), None),
        P(("dp", "tp")),
        P(("dp", "tp")),
        P(("dp", "tp")),
        P(("dp", "tp")),
        P("dp", "tp"),
        P("tp", None),
    )
    return jax.shard_map(
        shards,
        mesh=mesh,
        in_specs=placed,
        out_specs=(P(("dp", "tp"), None), P(("dp", "tp"), None)),
        check_vma=False,
    )
```
